32 devices in a mesh: parts: 2 (over x), dp: 2 (over core), tensor: 8 (over z, y).
Axes of the slice: x: 2, y: 2, z: 4, core: 2. Of those that a mesh axis runs over, the one named last changes fastest.
Arguments:
- tokens: bfloat16 [2048, 8192], P(('parts', 'dp'), 'tensor'), parts along dimension 0, may hold values from -6 to 6
- cotangent: bfloat16 [2048, 8192], P(('parts', 'dp'), 'tensor'), parts along dimension 0, may hold values from -6 to 6
- gate_weight: bfloat16 [8192, 14336], P('dp', 'tensor'), may hold values from -0.0625 to 0.0625
- up_weight: bfloat16 [8192, 14336], P('dp', 'tensor'), may hold values from -0.0625 to 0.0625
- down_weight: bfloat16 [14336, 8192], P('tensor', 'dp'), may hold values from -0.0625 to 0.0625
- proj_tokens: bfloat16 [8192, 64], P('tensor'), may hold values from -0.0625 to 0.0625
- proj_cotangent: bfloat16 [8192, 64], P('tensor'), may hold values from -0.0625 to 0.0625
- proj_hidden: bfloat16 [14336, 64], P('tensor'), may hold values from -0.046875 to 0.046875
- proj_gate: bfloat16 [14336, 64], P('tensor'), may hold values from -0.046875 to 0.046875
- proj_up: bfloat16 [14336, 64], P('tensor'), may hold values from -0.046875 to 0.046875
- doc_ids: int32 [4, 512], P(('parts', 'dp')), parts along dimension 0, may hold values from 0 to 7, never falling along the last dimension, each value on 1 to 256 neighbouring positions
- query_grads: bfloat16 [512, 12288], P('tensor'), may hold values from -0.029907227 to 0.029907227
Outputs:
- scores: float32 [32, 512], P(('parts', 'dp'), 'tensor'), parts along dimension 0
The draws below stay inside these ranges and needn't reach their ends.
There are 2 independent parts, one for each index of `parts`. The reference program is written for one: setup_inputs(seed, part) draws one part's arguments, and reference() takes and returns one part's arrays. A program takes and returns all parts, laid end to end along the dimension named above; an argument that names none is the same for every part. Nothing has to cross between parts.
Inputs may be any that keep to these rules, and one draw needn't show every extreme that they name: `doc_ids`: within each group the ids never fall; every id names 1 to 256 rows, and one names exactly 256.
All inputs are finite; a program needn't handle non-finite values.
Results may differ from the reference program's by a relative error of at most 0.0028.
Values may be sent and summed in bfloat16 or wider, within the bound.
A program may use at most 320 MiB of HBM per device.

```python
import math
import jax
import jax.numpy as jnp
import numpy as np
from jax import lax

D = 8192
FF = 14336
RANK = 64
TOK_DEV = 512
DOCS = 8
QUERIES = 512
GROUPS = 2
TOKENS = 1024


def block_scale(stream_key, extent, split, least, top_value):
    loudness, own = 1.0, jax.random.fold_in(stream_key, 6)
    for axis_at, parts in split:
        draws = jnp.exp(jax.random.uniform(jax.random.fold_in(own, axis_at), (parts,), jnp.float32, least / len(split), top_value / len(split)))
        loudness = loudness * jnp.repeat(draws, extent[axis_at] // parts).reshape([-1 if axis == axis_at else 1 for axis in range(len(extent))])
    return loudness


def length_profile(number_of, total, reach, skew):
    portions = [(1 << 20) // math.isqrt(standing ** skew) + 1 for standing in range(2, number_of + 1)]
    spare, counts = total - reach - (number_of - 1), [1] * (number_of - 1)
    while spare > 0:
        candidates = [i for i in range(number_of - 1) if counts[i] < reach]
        pool, remaining = sum([portions[i] for i in candidates]), spare
        for i in candidates:
            extra = min(reach - counts[i], max(1, remaining * portions[i] // pool), spare)
            counts[i] = counts[i] + extra
            spare = spare - extra
    return np.array([reach] + counts)


def uneven_parts(rng, amount, total, bound, slope):
    if amount == 2:
        one = jax.random.randint(rng, (), max(1, total - bound), min(bound, total - 1) + 1)
        return jnp.stack([one, total - one])
    tallies = jnp.asarray(length_profile(amount, total, bound, slope), jnp.int32)
    couples = (amount - 1) // 2
    giver, receiver = tallies[1:1 + 2 * couples:2], tallies[2:2 + 2 * couples:2]
    slack = jnp.minimum(giver - 1, bound - receiver)
    passed = jax.random.randint(jax.random.fold_in(rng, 1), (couples,), 0, 1 << 20) % (slack + 1)
    tallies = tallies.at[1:1 + 2 * couples:2].set(giver - passed).at[2:2 + 2 * couples:2].set(receiver + passed)
    return tallies[jax.random.permutation(jax.random.fold_in(rng, 2), amount)]


def noise(rng, extent, deviation, reach, cuts=(), kind=jnp.bfloat16):
    level = block_scale(rng, extent, cuts, -0.22, 0.18) if cuts else 1.0
    entries = jax.random.normal(rng, extent, jnp.float32) * deviation * level
    return jnp.minimum(jnp.maximum(entries, -reach), reach).astype(kind)


def setup_inputs(seed: int = 0, part: int = 0) -> dict:
    arg_keys = jax.random.split(jax.random.key(seed), 13)
    part_keys = jax.random.split(jax.random.fold_in(arg_keys[12], part), 13)
    return {
        "tokens": noise(part_keys[0], (TOKENS, D), 1.0, 6.0, ((0, 2), (1, 8))),
        "cotangent": noise(part_keys[1], (TOKENS, D), 1.0, 6.0, ((0, 2), (1, 8))),
        "gate_weight": noise(arg_keys[2], (D, FF), D ** -0.5, 0.0625, ((0, 2), (1, 8))),
        "up_weight": noise(arg_keys[3], (D, FF), D ** -0.5, 0.0625, ((0, 2), (1, 8))),
        "down_weight": noise(arg_keys[4], (FF, D), D ** -0.5, 0.0625, ((0, 8), (1, 2))),
        "proj_tokens": noise(arg_keys[5], (D, RANK), D ** -0.5, 0.0625, ((0, 8),)),
        "proj_cotangent": noise(arg_keys[6], (D, RANK), D ** -0.5, 0.0625, ((0, 8),)),
        "proj_hidden": noise(arg_keys[7], (FF, RANK), FF ** -0.5, 0.046875, ((0, 8),)),
        "proj_gate": noise(arg_keys[8], (FF, RANK), FF ** -0.5, 0.046875, ((0, 8),)),
        "proj_up": noise(arg_keys[9], (FF, RANK), FF ** -0.5, 0.046875, ((0, 8),)),
        "doc_ids": jax.vmap(lambda own: jnp.searchsorted(jnp.cumsum(uneven_parts(own, DOCS, TOK_DEV, TOK_DEV // 2, 2)), jnp.arange(TOK_DEV), side="right"))(jax.random.split(part_keys[10], GROUPS)).reshape((GROUPS, TOK_DEV)).astype(jnp.int32),
        "query_grads": noise(arg_keys[11], (QUERIES, 3 * RANK * RANK), 0.004, 0.029907227, ((0, 8),)),
    }


def outer_sums(onehot, left, right):
    weighted = (onehot[:, :, None] * left[:, None, :]).reshape(left.shape[0], -1)
    block = lax.dot_general(weighted, right, (((0,), (0,)), ((), ())), precision=lax.Precision.HIGHEST, preferred_element_type=jnp.float32)
    return block.reshape(onehot.shape[1], -1)


def group_factors(projected, doc_rows):
    onehot = (doc_rows[:, None] == jnp.arange(DOCS, dtype=jnp.int32)[None, :]).astype(jnp.float32)
    p_tokens = projected[:, 0:RANK]
    p_cotan = projected[:, RANK:2 * RANK]
    p_hidden = projected[:, 2 * RANK:3 * RANK]
    p_gate = projected[:, 3 * RANK:4 * RANK]
    p_upgrad = projected[:, 4 * RANK:5 * RANK]
    return jnp.concatenate([outer_sums(onehot, p_gate, p_tokens), outer_sums(onehot, p_upgrad, p_tokens), outer_sums(onehot, p_cotan, p_hidden)], axis=1)


def reference(tokens, cotangent, gate_weight, up_weight, down_weight, proj_tokens, proj_cotangent, proj_hidden, proj_gate, proj_up, doc_ids, query_grads):
    gate_pre = jnp.dot(tokens, gate_weight, preferred_element_type=jnp.float32)
    up_pre = jnp.dot(tokens, up_weight, preferred_element_type=jnp.float32)
    sigmoid_gate = jax.nn.sigmoid(gate_pre)
    hidden = (gate_pre * sigmoid_gate * up_pre).astype(jnp.bfloat16)
    grad_hidden = jnp.dot(cotangent, down_weight.T, preferred_element_type=jnp.float32)
    grad_up = (grad_hidden * gate_pre * sigmoid_gate).astype(jnp.bfloat16)
    grad_gate = (grad_hidden * up_pre * sigmoid_gate * (1.0 + gate_pre * (1.0 - sigmoid_gate))).astype(jnp.bfloat16)
    projected = jnp.concatenate([
        jnp.dot(tokens, proj_tokens, preferred_element_type=jnp.float32),
        jnp.dot(cotangent, proj_cotangent, preferred_element_type=jnp.float32),
        jnp.dot(hidden, proj_hidden, preferred_element_type=jnp.float32),
        jnp.dot(grad_gate, proj_gate, preferred_element_type=jnp.float32),
        jnp.dot(grad_up, proj_up, preferred_element_type=jnp.float32)], axis=1)
    grouped = projected.reshape(GROUPS, TOK_DEV, 5 * RANK)
    factors = jax.vmap(group_factors)(grouped, doc_ids).reshape(GROUPS * DOCS, 3 * RANK * RANK)
    return jnp.dot(factors, query_grads.astype(jnp.float32).T, precision=lax.Precision.HIGHEST, preferred_element_type=jnp.float32)
```

```python
import functools

import jax
import jax.numpy as jnp
from jax import lax
from jax.experimental import pallas as pl
from jax.experimental.pallas import tpu as pltpu
from jax.sharding import PartitionSpec as P

RANK = 64
DOCS = 8
PIECES = 4
MESH = pl.DeviceIdType.MESH


def outer_sums(onehot, left, right):
    weighted = (onehot[:, :, None] * left[:, None, :]).reshape(left.shape[0], -1)
    block = lax.dot_general(
        weighted,
        right,
        (((0,), (0,)), ((), ())),
        precision=lax.Precision.HIGHEST,
        preferred_element_type=jnp.float32,
    )
    return block.reshape(onehot.shape[1], -1)


def group_factors(projected, doc_rows):
    onehot = (doc_rows[:, None] == jnp.arange(DOCS, dtype=jnp.int32)[None, :]).astype(jnp.float32)
    p_tokens = projected[:, 0:RANK]
    p_cotan = projected[:, RANK : 2 * RANK]
    p_gate = projected[:, 2 * RANK : 3 * RANK]
    p_upgrad = projected[:, 3 * RANK : 4 * RANK]
    p_hidden = projected[:, 4 * RANK : 5 * RANK]
    return jnp.concatenate(
        [
            outer_sums(onehot, p_gate, p_tokens),
            outer_sums(onehot, p_upgrad, p_tokens),
            outer_sums(onehot, p_cotan, p_hidden),
        ],
        axis=1,
    )


def kernel(
    tensor, rows, feats, units, tile,
    tok_ref, cot_ref, gw_ref, uw_ref, dw_ref, ph_ref, pgate_ref, pup_ref, xpg_ref,
    out_ref,
    got, acc_g, acc_u, acc_h, swapped, gbuf, ubuf, dbuf, part, parts_in,
    swap_send, swap_recv, local_sem, z_up, z_down, z_recv, y_send, y_recv,
    w_sem, x_send, x_recv, x_free, rs_send, rs_recv, ag_send, ag_recv,
):
    n = tensor // 4
    planes = tensor // 2
    piece = rows * 2 // PIECES
    per_group = PIECES // 2
    tiles = units // tile
    own_rows = rows // tensor
    t = lax.axis_index("tensor")
    d = lax.axis_index("dp")
    z, y = t // 2, t % 2
    half = t // (2 * n)
    is_src = half == d
    own_blk = t - half * (2 * n)
    near = jnp.clip(z - d * n, 0, n - 1)

    def peer(k):
        return lax.rem(t + k, tensor)

    def column(i):
        return lax.rem(near - i + n, n)

    barrier = pltpu.get_barrier_semaphore()
    pl.semaphore_signal(barrier, inc=1, device_id={"dp": 1 - d}, device_id_type=MESH)
    for k in range(1, tensor):
        pl.semaphore_signal(barrier, inc=1, device_id={"tensor": peer(k)}, device_id_type=MESH)

    def w_gate(blk):
        return pltpu.make_async_copy(gw_ref.at[pl.ds(blk * feats, feats)], gbuf, w_sem.at[0])

    def w_up(blk):
        return pltpu.make_async_copy(uw_ref.at[pl.ds(blk * feats, feats)], ubuf, w_sem.at[1])

    def w_down(blk):
        at = pl.multiple_of(blk * feats, feats)
        return pltpu.make_async_copy(dw_ref.at[:, pl.ds(at, feats)], dbuf, w_sem.at[2])

    def blk_own(i):
        return column(i) * 2 + y

    def blk_cross(i):
        return column(i) * 2 + 1 - y

    w_gate(blk_own(0)).start()
    w_up(blk_own(0)).start()
    w_down(blk_own(0)).start()

    srcs = (tok_ref, cot_ref)

    def local(a):
        return pltpu.make_async_copy(srcs[a], got.at[a, own_blk, d], local_sem.at[a])

    def swap(a, group):
        return pltpu.make_async_remote_copy(
            src_ref=srcs[a], dst_ref=got.at[a, own_blk, group],
            send_sem=swap_send.at[a], recv_sem=swap_recv.at[a],
            device_id={"dp": 1 - d}, device_id_type=MESH,
        )

    @pl.when(is_src)
    def _():
        for a in range(2):
            local(a).start()

    pl.semaphore_wait(barrier, tensor)

    @pl.when(jnp.logical_not(is_src))
    def _():
        for a in range(2):
            swap(a, d).start()

    def where(a, c, yy, p):
        return got.at[a, c * 2 + yy, p // per_group, pl.ds((p % per_group) * piece, piece)]

    def sem_at(a, c, p):
        return (a * n + c) * PIECES + p

    def z_copy(a, c, p, up):
        ref = where(a, c, y, p)
        step = 2 if up else -2
        return pltpu.make_async_remote_copy(
            src_ref=ref, dst_ref=ref,
            send_sem=(z_up if up else z_down).at[sem_at(a, c, p)],
            recv_sem=z_recv.at[sem_at(a, c, p)],
            device_id={"tensor": lax.rem(t + step + tensor, tensor)}, device_id_type=MESH,
        )

    def y_copy(a, c, yy, p):
        ref = where(a, c, yy, p)
        return pltpu.make_async_remote_copy(
            src_ref=ref, dst_ref=ref,
            send_sem=y_send.at[sem_at(a, c, p)],
            recv_sem=y_recv.at[sem_at(a, c, p)],
            device_id={"tensor": t + 1 - 2 * y}, device_id_type=MESH,
        )

    def goes_up(c):
        return jnp.logical_and(z >= d * n + c, z < planes - 1)

    def goes_down(c):
        return jnp.logical_and(z <= d * n + c, z > 0)

    def comm(a, i, first):
        c = column(i)
        if first:
            @pl.when(is_src)
            def _():
                local(a).wait()
                swap(a, 1 - d).wait_recv()

        for p in range(PIECES):
            @pl.when(z != d * n + c)
            def _():
                z_copy(a, c, p, True).wait_recv()

            @pl.when(goes_up(c))
            def _():
                z_copy(a, c, p, True).start()

            @pl.when(goes_down(c))
            def _():
                z_copy(a, c, p, False).start()

            y_copy(a, c, y, p).start()

    def wait_cross(a, i):
        for p in range(PIECES):
            y_copy(a, column(i), 1 - y, p).wait_recv()

    def add_tokens(blk):
        def body(k, carry):
            g, j = k // tiles, k % tiles
            at = pl.ds(pl.multiple_of(j * tile, tile), tile)
            x = got[0, blk, g]
            acc_g[g, :, at] += jnp.dot(x, gbuf[:, at], preferred_element_type=jnp.float32)
            acc_u[g, :, at] += jnp.dot(x, ubuf[:, at], preferred_element_type=jnp.float32)
            return carry

        w_gate(blk).wait()
        w_up(blk).wait()
        lax.fori_loop(0, 2 * tiles, body, 0)

    def add_cotangent(blk):
        def body(k, carry):
            g, j = k // tiles, k % tiles
            start = pl.multiple_of(j * tile, tile)
            at = pl.ds(start, tile)
            acc_h[g, :, at] += lax.dot_general(
                got[1, blk, g], dbuf[at, :], (((1,), (1,)), ((), ())),
                preferred_element_type=jnp.float32,
            )
            return carry

        w_down(blk).wait()
        lax.fori_loop(0, 2 * tiles, body, 0)

    def next_tokens(blk):
        w_gate(blk).start()
        w_up(blk).start()

    def clear(j, carry):
        at = pl.ds(pl.multiple_of(j * tile, tile), tile)
        for g in range(2):
            zero = jnp.zeros((rows, tile), jnp.float32)
            acc_g[g, :, at] = zero
            acc_u[g, :, at] = zero
            acc_h[g, :, at] = zero
        return carry

    lax.fori_loop(0, tiles, clear, 0)
    part[:, 0:128] = xpg_ref[...]
    part[:, 128:384] = jnp.zeros((rows, 256), jnp.float32)

    def exchange(k):
        return pltpu.make_async_remote_copy(
            src_ref=(acc_g, acc_u, acc_h)[k].at[1 - d], dst_ref=swapped.at[k % 2],
            send_sem=x_send.at[k], recv_sem=x_recv.at[k],
            device_id={"dp": 1 - d}, device_id_type=MESH,
        )

    comm(0, 0, True)
    add_tokens(blk_own(0))

    def token_step(i, carry):
        next_tokens(blk_own(i))
        comm(0, i, False)
        add_tokens(blk_own(i))
        next_tokens(blk_cross(i - 1))
        wait_cross(0, i - 1)
        add_tokens(blk_cross(i - 1))
        return carry

    lax.fori_loop(1, n, token_step, 0)
    next_tokens(blk_cross(n - 1))

    comm(1, 0, True)
    add_cotangent(blk_own(0))
    wait_cross(0, n - 1)
    add_tokens(blk_cross(n - 1))
    exchange(0).start()
    exchange(1).start()

    def cotangent_step(i, carry):
        w_down(blk_own(i)).start()
        comm(1, i, False)
        add_cotangent(blk_own(i))
        w_down(blk_cross(i - 1)).start()
        wait_cross(1, i - 1)
        add_cotangent(blk_cross(i - 1))
        return carry

    lax.fori_loop(1, n, cotangent_step, 0)
    w_down(blk_cross(n - 1)).start()

    exchange(0).wait_recv()
    exchange(1).wait_recv()

    def activate(j, carry):
        at = pl.ds(pl.multiple_of(j * tile, tile), tile)
        gate = acc_g[d, :, at] + swapped[0, :, at]
        up = acc_u[d, :, at] + swapped[1, :, at]
        s = jax.nn.sigmoid(gate)
        silu = gate * s
        acc_g[d, :, at] = silu
        acc_u[d, :, at] = up * s * (1.0 + gate * (1.0 - s))
        hidden = (silu * up).astype(jnp.bfloat16)
        part[:, 256:384] += jnp.dot(hidden, ph_ref[at, :], preferred_element_type=jnp.float32)
        return carry

    lax.fori_loop(0, tiles, activate, 0)
    pl.semaphore_signal(x_free, inc=1, device_id={"dp": 1 - d}, device_id_type=MESH)

    wait_cross(1, n - 1)
    add_cotangent(blk_cross(n - 1))
    pl.semaphore_wait(x_free, 1)
    exchange(2).start()
    exchange(2).wait_recv()

    def gradients(j, carry):
        at = pl.ds(pl.multiple_of(j * tile, tile), tile)
        grad = acc_h[d, :, at] + swapped[0, :, at]
        grad_up = (grad * acc_g[d, :, at]).astype(jnp.bfloat16)
        grad_gate = (grad * acc_u[d, :, at]).astype(jnp.bfloat16)
        part[:, 128:256] += jnp.dot(
            grad_gate, pgate_ref[at, :], preferred_element_type=jnp.float32
        ) + jnp.dot(grad_up, pup_ref[at, :], preferred_element_type=jnp.float32)
        return carry

    lax.fori_loop(0, tiles, gradients, 0)

    def rs_copy(k):
        return pltpu.make_async_remote_copy(
            src_ref=part.at[pl.ds(pl.multiple_of(peer(k) * own_rows, own_rows), own_rows)],
            dst_ref=parts_in.at[k - 1],
            send_sem=rs_send.at[k - 1], recv_sem=rs_recv.at[k - 1],
            device_id={"tensor": peer(k)}, device_id_type=MESH,
        )

    def ag_copy(k, owner):
        ref = out_ref.at[pl.ds(pl.multiple_of(owner * own_rows, own_rows), own_rows)]
        return pltpu.make_async_remote_copy(
            src_ref=ref, dst_ref=ref,
            send_sem=ag_send.at[k - 1], recv_sem=ag_recv.at[k - 1],
            device_id={"tensor": peer(k)}, device_id_type=MESH,
        )

    mine = pl.ds(pl.multiple_of(t * own_rows, own_rows), own_rows)
    for k in range(1, tensor):
        rs_copy(k).start()
    total = part[mine, :]
    for k in range(1, tensor):
        rs_copy(k).wait_recv()
        total += parts_in[k - 1]
    out_ref[mine, :] = total
    for k in range(1, tensor):
        ag_copy(k, t).start()
    for k in range(1, tensor):
        ag_copy(k, peer(tensor - k)).wait_recv()

    for k in range(1, tensor):
        rs_copy(k).wait_send()
        ag_copy(k, t).wait_send()
    for k in range(3):
        exchange(k).wait_send()

    @pl.when(jnp.logical_not(is_src))
    def _():
        for a in range(2):
            swap(a, d).wait_send()

    def drain(c, carry):
        for a in range(2):
            for p in range(PIECES):
                @pl.when(goes_up(c))
                def _():
                    z_copy(a, c, p, True).wait_send()

                @pl.when(goes_down(c))
                def _():
                    z_copy(a, c, p, False).wait_send()

                y_copy(a, c, y, p).wait_send()
        return carry

    lax.fori_loop(0, n, drain, 0)


def projected_rows(tensor, tokens, cotangent, gate_weight, up_weight, down_weight, ph, pgate, pup, xpg):
    rows, feats = tokens.shape
    units = gate_weight.shape[1]
    tile = 256 if units % 256 == 0 else units
    n = tensor // 4
    steps = 2 * n * PIECES
    anywhere = pl.BlockSpec(memory_space=pl.ANY)
    vmem = pl.BlockSpec(memory_space=pltpu.VMEM)
    dma = pltpu.SemaphoreType.DMA
    f32, bf16 = jnp.float32, jnp.bfloat16
    return pl.pallas_call(
        functools.partial(kernel, tensor, rows, feats, units, tile),
        out_shape=jax.ShapeDtypeStruct((rows, 384), f32),
        in_specs=[anywhere] * 5 + [vmem] * 4,
        out_specs=vmem,
        scratch_shapes=[
            pltpu.VMEM((2, 2 * n, 2, rows, feats), bf16),
            pltpu.VMEM((2, rows, units), f32),
            pltpu.VMEM((2, rows, units), f32),
            pltpu.VMEM((2, rows, units), f32),
            pltpu.VMEM((2, rows, units), f32),
            pltpu.VMEM((feats, units), bf16),
            pltpu.VMEM((feats, units), bf16),
            pltpu.VMEM((units, feats), bf16),
            pltpu.VMEM((rows, 384), f32),
            pltpu.VMEM((tensor - 1, rows // tensor, 384), f32),
            dma((2,)), dma((2,)), dma((2,)),
            dma((steps,)), dma((steps,)), dma((steps,)), dma((steps,)), dma((steps,)),
            dma((3,)), dma((3,)), dma((3,)), pltpu.SemaphoreType.REGULAR,
            dma((tensor - 1,)), dma((tensor - 1,)), dma((tensor - 1,)), dma((tensor - 1,)),
        ],
        compiler_params=pltpu.CompilerParams(
            collective_id=0, has_side_effects=True, vmem_limit_bytes=61 * 1024 * 1024
        ),
    )(tokens, cotangent, gate_weight, up_weight, down_weight, ph, pgate, pup, xpg)


def local(
    tensor,
    tokens,
    cotangent,
    gate_weight,
    up_weight,
    down_weight,
    proj_tokens,
    proj_cotangent,
    proj_hidden,
    proj_gate,
    proj_up,
    doc_ids,
    query_grads,
):
    xpg = jnp.concatenate(
        [
            jnp.dot(tokens, proj_tokens, preferred_element_type=jnp.float32),
            jnp.dot(cotangent, proj_cotangent, preferred_element_type=jnp.float32),
        ],
        axis=1,
    )
    summed = projected_rows(
        tensor, tokens, cotangent, gate_weight, up_weight, down_weight,
        jnp.pad(proj_hidden, ((0, 0), (0, RANK))), jnp.pad(proj_gate, ((0, 0), (0, RANK))),
        jnp.pad(proj_up, ((0, 0), (RANK, 0))), xpg,
    )
    factors = group_factors(summed, doc_ids[0])
    return jnp.dot(
        factors,
        query_grads.astype(jnp.float32).T,
        precision=lax.Precision.HIGHEST,
        preferred_element_type=jnp.float32,
    )


def solution(mesh):
    return jax.shard_map(
        functools.partial(local, mesh.shape["tensor"]),
        mesh=mesh,
        in_specs=(
            P(("parts", "dp"), "tensor"),
            P(("parts", "dp"), "tensor"),
            P("dp", "tensor"),
            P("dp", "tensor"),
            P("tensor", "dp"),
            P("tensor", None),
            P("tensor", None),
            P("tensor", None),
            P("tensor", None),
            P("tensor", None),
            P(("parts", "dp"), None),
            P("tensor", None),
        ),
        out_specs=P(("parts", "dp"), "tensor"),
        check_vma=False,
    )
```

```python
import functools

import jax
import jax.numpy as jnp
from jax import lax
from jax.experimental import pallas as pl
from jax.experimental.pallas import tpu as pltpu
from jax.sharding import PartitionSpec as P

RANK = 64
DOCS = 8
PIECES = 4
MESH = pl.DeviceIdType.MESH


def outer_sums(onehot, left, right):
    weighted = (onehot[:, :, None] * left[:, None, :]).reshape(left.shape[0], -1)
    block = lax.dot_general(
        weighted,
        right,
        (((0,), (0,)), ((), ())),
        precision=lax.Precision.HIGHEST,
        preferred_element_type=jnp.float32,
    )
    return block.reshape(onehot.shape[1], -1)


def group_factors(projected, doc_rows):
    onehot = (doc_rows[:, None] == jnp.arange(DOCS, dtype=jnp.int32)[None, :]).astype(jnp.float32)
    p_tokens = projected[:, 0:RANK]
    p_cotan = projected[:, RANK : 2 * RANK]
    p_gate = projected[:, 2 * RANK : 3 * RANK]
    p_upgrad = projected[:, 3 * RANK : 4 * RANK]
    p_hidden = projected[:, 4 * RANK : 5 * RANK]
    return jnp.concatenate(
        [
            outer_sums(onehot, p_gate, p_tokens),
            outer_sums(onehot, p_upgrad, p_tokens),
            outer_sums(onehot, p_cotan, p_hidden),
        ],
        axis=1,
    )


def kernel(
    tensor, rows, feats, units, tile,
    tok_ref, cot_ref, gw_ref, uw_ref, dw_ref, ph_ref, pgate_ref, pup_ref, xpg_ref,
    out_ref,
    got, acc_g, acc_u, acc_h, swapped, gbuf, ubuf, dbuf, part, parts_in,
    swap_send, swap_recv, local_sem, z_up, z_down, z_recv, y_send, y_recv, s_send, s_recv,
    w_sem, x_send, x_recv, x_free, rs_send, rs_recv, ag_send, ag_recv,
):
    n = tensor // 4
    planes = tensor // 2
    piece = rows * 2 // PIECES
    per_group = PIECES // 2
    tiles = units // tile
    own_rows = rows // tensor
    t = lax.axis_index("tensor")
    d = lax.axis_index("dp")
    z, y = t // 2, t % 2
    half = t // (2 * n)
    is_src = half == d
    own_blk = t - half * (2 * n)
    near = jnp.clip(z - d * n, 0, n - 1)

    def peer(k):
        return lax.rem(t + k, tensor)

    def column(i):
        return lax.rem(near - i + n, n)

    barrier = pltpu.get_barrier_semaphore()
    pl.semaphore_signal(barrier, inc=1, device_id={"dp": 1 - d}, device_id_type=MESH)
    for k in range(1, tensor):
        pl.semaphore_signal(barrier, inc=1, device_id={"tensor": peer(k)}, device_id_type=MESH)

    def w_gate(blk):
        return pltpu.make_async_copy(gw_ref.at[pl.ds(blk * feats, feats)], gbuf, w_sem.at[0])

    def w_up(blk):
        return pltpu.make_async_copy(uw_ref.at[pl.ds(blk * feats, feats)], ubuf, w_sem.at[1])

    def w_down(blk):
        at = pl.multiple_of(blk * feats, feats)
        return pltpu.make_async_copy(dw_ref.at[:, pl.ds(at, feats)], dbuf, w_sem.at[2])

    def blk_own(i):
        return column(i) * 2 + y

    def blk_cross(i):
        return column(i) * 2 + 1 - y

    w_gate(blk_own(0)).start()
    w_up(blk_own(0)).start()
    w_down(blk_own(0)).start()

    srcs = (tok_ref, cot_ref)

    def local(a):
        return pltpu.make_async_copy(srcs[a], got.at[a, own_blk, d], local_sem.at[a])

    def swap(a, group):
        return pltpu.make_async_remote_copy(
            src_ref=srcs[a], dst_ref=got.at[a, own_blk, group],
            send_sem=swap_send.at[a], recv_sem=swap_recv.at[a],
            device_id={"dp": 1 - d}, device_id_type=MESH,
        )

    @pl.when(is_src)
    def _():
        for a in range(2):
            local(a).start()

    pl.semaphore_wait(barrier, tensor)

    @pl.when(jnp.logical_not(is_src))
    def _():
        for a in range(2):
            swap(a, d).start()

    def where(a, c, yy, p):
        return got.at[a, c * 2 + yy, p // per_group, pl.ds((p % per_group) * piece, piece)]

    def sem_at(a, c, p):
        return (a * n + c) * PIECES + p

    def z_copy(a, c, p, up):
        ref = where(a, c, y, p)
        step = 2 if up else -2
        return pltpu.make_async_remote_copy(
            src_ref=ref, dst_ref=ref,
            send_sem=(z_up if up else z_down).at[sem_at(a, c, p)],
            recv_sem=z_recv.at[sem_at(a, c, p)],
            device_id={"tensor": lax.rem(t + step + tensor, tensor)}, device_id_type=MESH,
        )

    def y_copy(a, c, yy, p):
        ref = where(a, c, yy, p)
        return pltpu.make_async_remote_copy(
            src_ref=ref, dst_ref=ref,
            send_sem=y_send.at[sem_at(a, c, p)],
            recv_sem=y_recv.at[sem_at(a, c, p)],
            device_id={"tensor": t + 1 - 2 * y}, device_id_type=MESH,
        )

    def goes_up(c):
        return jnp.logical_and(z >= d * n + c, z < planes - 1)

    def goes_down(c):
        return jnp.logical_and(z <= d * n + c, z > 0)

    def comm(a, i, first):
        c = column(i)
        if first:
            @pl.when(is_src)
            def _():
                local(a).wait()
                swap(a, 1 - d).wait_recv()

        for p in range(PIECES):
            @pl.when(z != d * n + c)
            def _():
                z_copy(a, c, p, True).wait_recv()

            @pl.when(goes_up(c))
            def _():
                z_copy(a, c, p, True).start()

            @pl.when(goes_down(c))
            def _():
                z_copy(a, c, p, False).start()

            if p < PIECES // 2:
                y_copy(a, c, y, p).start()
            else:
                @pl.when(crosses(c))
                def _():
                    y_copy(a, c, y, p).start()

    end_c = d * (n - 1)
    end_z = d * (planes - 1)
    last_z = (planes - 1) - end_z

    def crosses(c):
        return jnp.logical_or(c != end_c, z == end_z)

    def side_copy(a, p):
        ref = where(a, end_c, 1 - y, p)
        to = jnp.clip(t + 2 - 4 * d, 0, tensor - 1)
        q = a * (PIECES // 2) + p - PIECES // 2
        return pltpu.make_async_remote_copy(
            src_ref=ref, dst_ref=ref, send_sem=s_send.at[q], recv_sem=s_recv.at[q],
            device_id={"tensor": to}, device_id_type=MESH,
        )

    def wait_cross(a, i):
        c = column(i)
        for p in range(PIECES // 2, PIECES):
            @pl.when(crosses(c))
            def _():
                y_copy(a, c, 1 - y, p).wait_recv()

            @pl.when(jnp.logical_not(crosses(c)))
            def _():
                side_copy(a, p).wait_recv()

            @pl.when(jnp.logical_and(c == end_c, z != last_z))
            def _():
                side_copy(a, p).start()

        for p in range(PIECES // 2):
            y_copy(a, c, 1 - y, p).wait_recv()

    def add_tokens(blk):
        def body(k, carry):
            g, j = k // tiles, k % tiles
            at = pl.ds(pl.multiple_of(j * tile, tile), tile)
            x = got[0, blk, g]
            acc_g[g, :, at] += jnp.dot(x, gbuf[:, at], preferred_element_type=jnp.float32)
            acc_u[g, :, at] += jnp.dot(x, ubuf[:, at], preferred_element_type=jnp.float32)
            return carry

        w_gate(blk).wait()
        w_up(blk).wait()
        lax.fori_loop(0, 2 * tiles, body, 0)

    def add_cotangent(blk):
        def body(k, carry):
            g, j = k // tiles, k % tiles
            start = pl.multiple_of(j * tile, tile)
            at = pl.ds(start, tile)
            acc_h[g, :, at] += lax.dot_general(
                got[1, blk, g], dbuf[at, :], (((1,), (1,)), ((), ())),
                preferred_element_type=jnp.float32,
            )
            return carry

        w_down(blk).wait()
        lax.fori_loop(0, 2 * tiles, body, 0)

    def next_tokens(blk):
        w_gate(blk).start()
        w_up(blk).start()

    def clear(j, carry):
        at = pl.ds(pl.multiple_of(j * tile, tile), tile)
        for g in range(2):
            zero = jnp.zeros((rows, tile), jnp.float32)
            acc_g[g, :, at] = zero
            acc_u[g, :, at] = zero
            acc_h[g, :, at] = zero
        return carry

    lax.fori_loop(0, tiles, clear, 0)
    part[:, 0:128] = xpg_ref[...]
    part[:, 128:384] = jnp.zeros((rows, 256), jnp.float32)

    def exchange(k):
        return pltpu.make_async_remote_copy(
            src_ref=(acc_g, acc_u, acc_h)[k].at[1 - d], dst_ref=swapped.at[k % 2],
            send_sem=x_send.at[k], recv_sem=x_recv.at[k],
            device_id={"dp": 1 - d}, device_id_type=MESH,
        )

    comm(0, 0, True)
    add_tokens(blk_own(0))

    def token_step(i, carry):
        next_tokens(blk_own(i))
        comm(0, i, False)
        add_tokens(blk_own(i))
        next_tokens(blk_cross(i - 1))
        wait_cross(0, i - 1)
        add_tokens(blk_cross(i - 1))
        return carry

    lax.fori_loop(1, n, token_step, 0)
    next_tokens(blk_cross(n - 1))

    comm(1, 0, True)
    add_cotangent(blk_own(0))
    wait_cross(0, n - 1)
    add_tokens(blk_cross(n - 1))
    exchange(0).start()
    exchange(1).start()

    def cotangent_step(i, carry):
        w_down(blk_own(i)).start()
        comm(1, i, False)
        add_cotangent(blk_own(i))
        w_down(blk_cross(i - 1)).start()
        wait_cross(1, i - 1)
        add_cotangent(blk_cross(i - 1))
        return carry

    lax.fori_loop(1, n, cotangent_step, 0)
    w_down(blk_cross(n - 1)).start()

    exchange(0).wait_recv()
    exchange(1).wait_recv()

    def activate(j, carry):
        at = pl.ds(pl.multiple_of(j * tile, tile), tile)
        gate = acc_g[d, :, at] + swapped[0, :, at]
        up = acc_u[d, :, at] + swapped[1, :, at]
        s = jax.nn.sigmoid(gate)
        silu = gate * s
        acc_g[d, :, at] = silu
        acc_u[d, :, at] = up * s * (1.0 + gate * (1.0 - s))
        hidden = (silu * up).astype(jnp.bfloat16)
        part[:, 256:384] += jnp.dot(hidden, ph_ref[at, :], preferred_element_type=jnp.float32)
        return carry

    lax.fori_loop(0, tiles, activate, 0)
    pl.semaphore_signal(x_free, inc=1, device_id={"dp": 1 - d}, device_id_type=MESH)

    wait_cross(1, n - 1)
    add_cotangent(blk_cross(n - 1))
    pl.semaphore_wait(x_free, 1)
    exchange(2).start()
    exchange(2).wait_recv()

    def gradients(j, carry):
        at = pl.ds(pl.multiple_of(j * tile, tile), tile)
        grad = acc_h[d, :, at] + swapped[0, :, at]
        grad_up = (grad * acc_g[d, :, at]).astype(jnp.bfloat16)
        grad_gate = (grad * acc_u[d, :, at]).astype(jnp.bfloat16)
        part[:, 128:256] += jnp.dot(
            grad_gate, pgate_ref[at, :], preferred_element_type=jnp.float32
        ) + jnp.dot(grad_up, pup_ref[at, :], preferred_element_type=jnp.float32)
        return carry

    lax.fori_loop(0, tiles, gradients, 0)

    def rs_copy(k):
        return pltpu.make_async_remote_copy(
            src_ref=part.at[pl.ds(pl.multiple_of(peer(k) * own_rows, own_rows), own_rows)],
            dst_ref=parts_in.at[k - 1],
            send_sem=rs_send.at[k - 1], recv_sem=rs_recv.at[k - 1],
            device_id={"tensor": peer(k)}, device_id_type=MESH,
        )

    def ag_copy(k, owner):
        ref = out_ref.at[pl.ds(pl.multiple_of(owner * own_rows, own_rows), own_rows)]
        return pltpu.make_async_remote_copy(
            src_ref=ref, dst_ref=ref,
            send_sem=ag_send.at[k - 1], recv_sem=ag_recv.at[k - 1],
            device_id={"tensor": peer(k)}, device_id_type=MESH,
        )

    mine = pl.ds(pl.multiple_of(t * own_rows, own_rows), own_rows)
    for k in range(1, tensor):
        rs_copy(k).start()
    total = part[mine, :]
    for k in range(1, tensor):
        rs_copy(k).wait_recv()
        total += parts_in[k - 1]
    out_ref[mine, :] = total
    for k in range(1, tensor):
        ag_copy(k, t).start()
    for k in range(1, tensor):
        ag_copy(k, peer(tensor - k)).wait_recv()

    for k in range(1, tensor):
        rs_copy(k).wait_send()
        ag_copy(k, t).wait_send()
    for k in range(3):
        exchange(k).wait_send()

    @pl.when(jnp.logical_not(is_src))
    def _():
        for a in range(2):
            swap(a, d).wait_send()

    def drain(c, carry):
        for a in range(2):
            for p in range(PIECES):
                @pl.when(goes_up(c))
                def _():
                    z_copy(a, c, p, True).wait_send()

                @pl.when(goes_down(c))
                def _():
                    z_copy(a, c, p, False).wait_send()

                if p < PIECES // 2:
                    y_copy(a, c, y, p).wait_send()
                else:
                    @pl.when(crosses(c))
                    def _():
                        y_copy(a, c, y, p).wait_send()
        return carry

    lax.fori_loop(0, n, drain, 0)

    @pl.when(z != last_z)
    def _():
        for a in range(2):
            for p in range(PIECES // 2, PIECES):
                side_copy(a, p).wait_send()


def projected_rows(tensor, tokens, cotangent, gate_weight, up_weight, down_weight, ph, pgate, pup, xpg):
    rows, feats = tokens.shape
    units = gate_weight.shape[1]
    tile = 256 if units % 256 == 0 else units
    n = tensor // 4
    steps = 2 * n * PIECES
    anywhere = pl.BlockSpec(memory_space=pl.ANY)
    vmem = pl.BlockSpec(memory_space=pltpu.VMEM)
    dma = pltpu.SemaphoreType.DMA
    f32, bf16 = jnp.float32, jnp.bfloat16
    return pl.pallas_call(
        functools.partial(kernel, tensor, rows, feats, units, tile),
        out_shape=jax.ShapeDtypeStruct((rows, 384), f32),
        in_specs=[anywhere] * 5 + [vmem] * 4,
        out_specs=vmem,
        scratch_shapes=[
            pltpu.VMEM((2, 2 * n, 2, rows, feats), bf16),
            pltpu.VMEM((2, rows, units), f32),
            pltpu.VMEM((2, rows, units), f32),
            pltpu.VMEM((2, rows, units), f32),
            pltpu.VMEM((2, rows, units), f32),
            pltpu.VMEM((feats, units), bf16),
            pltpu.VMEM((feats, units), bf16),
            pltpu.VMEM((units, feats), bf16),
            pltpu.VMEM((rows, 384), f32),
            pltpu.VMEM((tensor - 1, rows // tensor, 384), f32),
            dma((2,)), dma((2,)), dma((2,)),
            dma((steps,)), dma((steps,)), dma((steps,)), dma((steps,)), dma((steps,)),
            dma((PIECES,)), dma((PIECES,)),
            dma((3,)), dma((3,)), dma((3,)), pltpu.SemaphoreType.REGULAR,
            dma((tensor - 1,)), dma((tensor - 1,)), dma((tensor - 1,)), dma((tensor - 1,)),
        ],
        compiler_params=pltpu.CompilerParams(
            collective_id=0, has_side_effects=True, vmem_limit_bytes=61 * 1024 * 1024
        ),
    )(tokens, cotangent, gate_weight, up_weight, down_weight, ph, pgate, pup, xpg)


def local(
    tensor,
    tokens,
    cotangent,
    gate_weight,
    up_weight,
    down_weight,
    proj_tokens,
    proj_cotangent,
    proj_hidden,
    proj_gate,
    proj_up,
    doc_ids,
    query_grads,
):
    xpg = jnp.concatenate(
        [
            jnp.dot(tokens, proj_tokens, preferred_element_type=jnp.float32),
            jnp.dot(cotangent, proj_cotangent, preferred_element_type=jnp.float32),
        ],
        axis=1,
    )
    summed = projected_rows(
        tensor, tokens, cotangent, gate_weight, up_weight, down_weight,
        jnp.pad(proj_hidden, ((0, 0), (0, RANK))), jnp.pad(proj_gate, ((0, 0), (0, RANK))),
        jnp.pad(proj_up, ((0, 0), (RANK, 0))), xpg,
    )
    factors = group_factors(summed, doc_ids[0])
    return jnp.dot(
        factors,
        query_grads.astype(jnp.float32).T,
        precision=lax.Precision.HIGHEST,
        preferred_element_type=jnp.float32,
    )


def solution(mesh):
    return jax.shard_map(
        functools.partial(local, mesh.shape["tensor"]),
        mesh=mesh,
        in_specs=(
            P(("parts", "dp"), "tensor"),
            P(("parts", "dp"), "tensor"),
            P("dp", "tensor"),
            P("dp", "tensor"),
            P("tensor", "dp"),
            P("tensor", None),
            P("tensor", None),
            P("tensor", None),
            P("tensor", None),
            P("tensor", None),
            P(("parts", "dp"), None),
            P("tensor", None),
        ),
        out_specs=P(("parts", "dp"), "tensor"),
        check_vma=False,
    )
```

```python
import functools

import jax
import jax.numpy as jnp
from jax import lax
from jax.experimental import pallas as pl
from jax.experimental.pallas import tpu as pltpu
from jax.sharding import PartitionSpec as P

RANK = 64
DOCS = 8
PIECES = 4
MESH = pl.DeviceIdType.MESH


def outer_sums(onehot, left, right):
    weighted = (onehot[:, :, None] * left[:, None, :]).reshape(left.shape[0], -1)
    block = lax.dot_general(
        weighted,
        right,
        (((0,), (0,)), ((), ())),
        precision=lax.Precision.HIGHEST,
        preferred_element_type=jnp.float32,
    )
    return block.reshape(onehot.shape[1], -1)


def group_factors(projected, doc_rows):
    onehot = (doc_rows[:, None] == jnp.arange(DOCS, dtype=jnp.int32)[None, :]).astype(jnp.float32)
    p_tokens = projected[:, 0:RANK]
    p_cotan = projected[:, RANK : 2 * RANK]
    p_gate = projected[:, 2 * RANK : 3 * RANK]
    p_upgrad = projected[:, 3 * RANK : 4 * RANK]
    p_hidden = projected[:, 4 * RANK : 5 * RANK]
    return jnp.concatenate(
        [
            outer_sums(onehot, p_gate, p_tokens),
            outer_sums(onehot, p_upgrad, p_tokens),
            outer_sums(onehot, p_cotan, p_hidden),
        ],
        axis=1,
    )


def kernel(
    tensor, rows, feats, units, tile,
    tok_ref, cot_ref, gw_ref, uw_ref, dw_ref, pt_in, pc_in, ph_in, pgate_in, pup_in,
    out_ref,
    got, acc_g, acc_u, acc_h, swapped, gbuf, dbuf, part, parts_in,
    xbuf, pt_ref, pc_ref, ph_ref, pgate_ref, pup_ref, in_sem,
    swap_send, swap_recv, local_sem, z_up, z_down, z_recv, y_send, y_recv, s_send, s_recv,
    w_sem, x_send, x_recv, x_free, rs_send, rs_recv, ag_send, ag_recv,
):
    n = tensor // 4
    planes = tensor // 2
    piece = rows * 2 // PIECES
    per_group = PIECES // 2
    tiles = units // tile
    own_rows = rows // tensor
    t = lax.axis_index("tensor")
    d = lax.axis_index("dp")
    z, y = t // 2, t % 2
    half = t // (2 * n)
    is_src = half == d
    own_blk = t - half * (2 * n)
    near = jnp.clip(z - d * n, 0, n - 1)

    def peer(k):
        return lax.rem(t + k, tensor)

    def column(i):
        return lax.rem(near - i + n, n)

    barrier = pltpu.get_barrier_semaphore()
    pl.semaphore_signal(barrier, inc=1, device_id={"dp": 1 - d}, device_id_type=MESH)
    for k in range(1, tensor):
        pl.semaphore_signal(barrier, inc=1, device_id={"tensor": peer(k)}, device_id_type=MESH)

    def w_gate(blk):
        return pltpu.make_async_copy(gw_ref.at[pl.ds(blk * feats, feats)], gbuf, w_sem.at[0])

    def w_up(blk):
        return pltpu.make_async_copy(uw_ref.at[pl.ds(blk * feats, feats)], gbuf, w_sem.at[1])

    def w_down(blk):
        at = pl.multiple_of(blk * feats, feats)
        return pltpu.make_async_copy(dw_ref.at[:, pl.ds(at, feats)], dbuf, w_sem.at[2])

    def blk_own(i):
        return column(i) * 2 + y

    def blk_cross(i):
        return column(i) * 2 + 1 - y

    w_gate(blk_own(0)).start()
    w_down(blk_own(0)).start()

    srcs = (tok_ref, cot_ref)
    projections = (
        (pt_in, pt_ref), (pc_in, pc_ref), (ph_in, ph_ref), (pgate_in, pgate_ref), (pup_in, pup_ref)
    )

    def load(k):
        return pltpu.make_async_copy(projections[k][0], projections[k][1], in_sem.at[k])

    def own_rows_in(a):
        return pltpu.make_async_copy(srcs[a], xbuf, in_sem.at[5 + a])

    for k in range(5):
        load(k).start()
    own_rows_in(0).start()

    def local(a):
        return pltpu.make_async_copy(srcs[a], got.at[a, own_blk, d], local_sem.at[a])

    def swap(a, group):
        return pltpu.make_async_remote_copy(
            src_ref=srcs[a], dst_ref=got.at[a, own_blk, group],
            send_sem=swap_send.at[a], recv_sem=swap_recv.at[a],
            device_id={"dp": 1 - d}, device_id_type=MESH,
        )

    @pl.when(is_src)
    def _():
        for a in range(2):
            local(a).start()

    pl.semaphore_wait(barrier, tensor)

    @pl.when(jnp.logical_not(is_src))
    def _():
        for a in range(2):
            swap(a, d).start()

    def where(a, c, yy, p):
        return got.at[a, c * 2 + yy, p // per_group, pl.ds((p % per_group) * piece, piece)]

    def sem_at(a, c, p):
        return (a * n + c) * PIECES + p

    def z_copy(a, c, p, up):
        ref = where(a, c, y, p)
        step = 2 if up else -2
        return pltpu.make_async_remote_copy(
            src_ref=ref, dst_ref=ref,
            send_sem=(z_up if up else z_down).at[sem_at(a, c, p)],
            recv_sem=z_recv.at[sem_at(a, c, p)],
            device_id={"tensor": lax.rem(t + step + tensor, tensor)}, device_id_type=MESH,
        )

    def y_copy(a, c, yy, p):
        ref = where(a, c, yy, p)
        return pltpu.make_async_remote_copy(
            src_ref=ref, dst_ref=ref,
            send_sem=y_send.at[sem_at(a, c, p)],
            recv_sem=y_recv.at[sem_at(a, c, p)],
            device_id={"tensor": t + 1 - 2 * y}, device_id_type=MESH,
        )

    def goes_up(c):
        return jnp.logical_and(z >= d * n + c, z < planes - 1)

    def goes_down(c):
        return jnp.logical_and(z <= d * n + c, z > 0)

    def comm(a, i, first):
        c = column(i)
        if first:
            @pl.when(is_src)
            def _():
                local(a).wait()
                swap(a, 1 - d).wait_recv()

        for p in range(PIECES):
            @pl.when(z != d * n + c)
            def _():
                z_copy(a, c, p, True).wait_recv()

            @pl.when(goes_up(c))
            def _():
                z_copy(a, c, p, True).start()

            @pl.when(goes_down(c))
            def _():
                z_copy(a, c, p, False).start()

            if p < PIECES // 2:
                y_copy(a, c, y, p).start()
            else:
                @pl.when(crosses(c))
                def _():
                    y_copy(a, c, y, p).start()

    end_c = d * (n - 1)
    end_z = d * (planes - 1)
    last_z = (planes - 1) - end_z

    def crosses(c):
        return jnp.logical_or(c != end_c, z == end_z)

    def side_copy(a, p):
        ref = where(a, end_c, 1 - y, p)
        to = jnp.clip(t + 2 - 4 * d, 0, tensor - 1)
        q = a * (PIECES // 2) + p - PIECES // 2
        return pltpu.make_async_remote_copy(
            src_ref=ref, dst_ref=ref, send_sem=s_send.at[q], recv_sem=s_recv.at[q],
            device_id={"tensor": to}, device_id_type=MESH,
        )

    def wait_cross(a, i):
        c = column(i)
        for p in range(PIECES // 2, PIECES):
            @pl.when(crosses(c))
            def _():
                y_copy(a, c, 1 - y, p).wait_recv()

            @pl.when(jnp.logical_not(crosses(c)))
            def _():
                side_copy(a, p).wait_recv()

            @pl.when(jnp.logical_and(c == end_c, z != last_z))
            def _():
                side_copy(a, p).start()

        for p in range(PIECES // 2):
            y_copy(a, c, 1 - y, p).wait_recv()

    def add_tokens(blk):
        def add_into(acc):
            def body(k, carry):
                g, j = k // tiles, k % tiles
                at = pl.ds(pl.multiple_of(j * tile, tile), tile)
                acc[g, :, at] += jnp.dot(
                    got[0, blk, g], gbuf[:, at], preferred_element_type=jnp.float32
                )
                return carry

            lax.fori_loop(0, 2 * tiles, body, 0)

        w_gate(blk).wait()
        add_into(acc_g)
        w_up(blk).start()
        w_up(blk).wait()
        add_into(acc_u)

    def add_cotangent(blk):
        def body(k, carry):
            g, j = k // tiles, k % tiles
            start = pl.multiple_of(j * tile, tile)
            at = pl.ds(start, tile)
            acc_h[g, :, at] += lax.dot_general(
                got[1, blk, g], dbuf[at, :], (((1,), (1,)), ((), ())),
                preferred_element_type=jnp.float32,
            )
            return carry

        w_down(blk).wait()
        lax.fori_loop(0, 2 * tiles, body, 0)

    def next_tokens(blk):
        w_gate(blk).start()

    def clear(j, carry):
        at = pl.ds(pl.multiple_of(j * tile, tile), tile)
        for g in range(2):
            zero = jnp.zeros((rows, tile), jnp.float32)
            acc_g[g, :, at] = zero
            acc_u[g, :, at] = zero
            acc_h[g, :, at] = zero
        return carry

    lax.fori_loop(0, tiles, clear, 0)
    part[...] = jnp.zeros_like(part)

    def exchange(k):
        return pltpu.make_async_remote_copy(
            src_ref=(acc_g, acc_u, acc_h)[k].at[1 - d], dst_ref=swapped.at[k % 2],
            send_sem=x_send.at[k], recv_sem=x_recv.at[k],
            device_id={"dp": 1 - d}, device_id_type=MESH,
        )

    comm(0, 0, True)
    for k in range(5):
        load(k).wait()
    own_rows_in(0).wait()
    px = jnp.dot(xbuf[...], pt_ref[...], preferred_element_type=jnp.float32)
    part[:, 0:128] = jnp.concatenate([px, jnp.zeros_like(px)], axis=1)
    own_rows_in(1).start()
    add_tokens(blk_own(0))
    own_rows_in(1).wait()
    pg = jnp.dot(xbuf[...], pc_ref[...], preferred_element_type=jnp.float32)
    part[:, 0:128] += jnp.concatenate([jnp.zeros_like(pg), pg], axis=1)

    def token_step(i, carry):
        next_tokens(blk_own(i))
        comm(0, i, False)
        add_tokens(blk_own(i))
        next_tokens(blk_cross(i - 1))
        wait_cross(0, i - 1)
        add_tokens(blk_cross(i - 1))
        return carry

    lax.fori_loop(1, n, token_step, 0)
    next_tokens(blk_cross(n - 1))

    comm(1, 0, True)
    add_cotangent(blk_own(0))
    wait_cross(0, n - 1)
    add_tokens(blk_cross(n - 1))
    exchange(0).start()
    exchange(1).start()

    def cotangent_step(i, carry):
        w_down(blk_own(i)).start()
        comm(1, i, False)
        add_cotangent(blk_own(i))
        w_down(blk_cross(i - 1)).start()
        wait_cross(1, i - 1)
        add_cotangent(blk_cross(i - 1))
        return carry

    lax.fori_loop(1, n, cotangent_step, 0)
    w_down(blk_cross(n - 1)).start()

    exchange(0).wait_recv()
    exchange(1).wait_recv()

    def activate(j, carry):
        at = pl.ds(pl.multiple_of(j * tile, tile), tile)
        gate = acc_g[d, :, at] + swapped[0, :, at]
        up = acc_u[d, :, at] + swapped[1, :, at]
        s = jax.nn.sigmoid(gate)
        silu = gate * s
        acc_g[d, :, at] = silu
        acc_u[d, :, at] = up * s * (1.0 + gate * (1.0 - s))
        hidden = (silu * up).astype(jnp.bfloat16)
        part[:, 256 : 256 + RANK] += jnp.dot(
            hidden, ph_ref[at, :], preferred_element_type=jnp.float32
        )
        return carry

    lax.fori_loop(0, tiles, activate, 0)
    pl.semaphore_signal(x_free, inc=1, device_id={"dp": 1 - d}, device_id_type=MESH)

    wait_cross(1, n - 1)
    add_cotangent(blk_cross(n - 1))
    pl.semaphore_wait(x_free, 1)
    exchange(2).start()
    exchange(2).wait_recv()

    def gradients(j, carry):
        at = pl.ds(pl.multiple_of(j * tile, tile), tile)
        grad = acc_h[d, :, at] + swapped[0, :, at]
        grad_up = (grad * acc_g[d, :, at]).astype(jnp.bfloat16)
        grad_gate = (grad * acc_u[d, :, at]).astype(jnp.bfloat16)
        part[:, 128:256] += jnp.concatenate(
            [
                jnp.dot(grad_gate, pgate_ref[at, :], preferred_element_type=jnp.float32),
                jnp.dot(grad_up, pup_ref[at, :], preferred_element_type=jnp.float32),
            ],
            axis=1,
        )
        return carry

    lax.fori_loop(0, tiles, gradients, 0)

    def rs_copy(k):
        return pltpu.make_async_remote_copy(
            src_ref=part.at[pl.ds(pl.multiple_of(peer(k) * own_rows, own_rows), own_rows)],
            dst_ref=parts_in.at[k - 1],
            send_sem=rs_send.at[k - 1], recv_sem=rs_recv.at[k - 1],
            device_id={"tensor": peer(k)}, device_id_type=MESH,
        )

    def ag_copy(k, owner):
        ref = out_ref.at[pl.ds(pl.multiple_of(owner * own_rows, own_rows), own_rows)]
        return pltpu.make_async_remote_copy(
            src_ref=ref, dst_ref=ref,
            send_sem=ag_send.at[k - 1], recv_sem=ag_recv.at[k - 1],
            device_id={"tensor": peer(k)}, device_id_type=MESH,
        )

    mine = pl.ds(pl.multiple_of(t * own_rows, own_rows), own_rows)
    for k in range(1, tensor):
        rs_copy(k).start()
    total = part[mine, :]
    for k in range(1, tensor):
        rs_copy(k).wait_recv()
        total += parts_in[k - 1]
    out_ref[mine, :] = total
    for k in range(1, tensor):
        ag_copy(k, t).start()
    for k in range(1, tensor):
        ag_copy(k, peer(tensor - k)).wait_recv()

    for k in range(1, tensor):
        rs_copy(k).wait_send()
        ag_copy(k, t).wait_send()
    for k in range(3):
        exchange(k).wait_send()

    @pl.when(jnp.logical_not(is_src))
    def _():
        for a in range(2):
            swap(a, d).wait_send()

    def drain(c, carry):
        for a in range(2):
            for p in range(PIECES):
                @pl.when(goes_up(c))
                def _():
                    z_copy(a, c, p, True).wait_send()

                @pl.when(goes_down(c))
                def _():
                    z_copy(a, c, p, False).wait_send()

                if p < PIECES // 2:
                    y_copy(a, c, y, p).wait_send()
                else:
                    @pl.when(crosses(c))
                    def _():
                        y_copy(a, c, y, p).wait_send()
        return carry

    lax.fori_loop(0, n, drain, 0)

    @pl.when(z != last_z)
    def _():
        for a in range(2):
            for p in range(PIECES // 2, PIECES):
                side_copy(a, p).wait_send()


def projected_rows(tensor, tokens, cotangent, gate_weight, up_weight, down_weight, pt, pc, ph, pgate, pup):
    rows, feats = tokens.shape
    units = gate_weight.shape[1]
    tile = 256 if units % 256 == 0 else units
    n = tensor // 4
    steps = 2 * n * PIECES
    anywhere = pl.BlockSpec(memory_space=pl.ANY)
    vmem = pl.BlockSpec(memory_space=pltpu.VMEM)
    dma = pltpu.SemaphoreType.DMA
    f32, bf16 = jnp.float32, jnp.bfloat16
    return pl.pallas_call(
        functools.partial(kernel, tensor, rows, feats, units, tile),
        out_shape=jax.ShapeDtypeStruct((rows, 384), f32),
        in_specs=[anywhere] * 10,
        out_specs=vmem,
        scratch_shapes=[
            pltpu.VMEM((2, 2 * n, 2, rows, feats), bf16),
            pltpu.VMEM((2, rows, units), f32),
            pltpu.VMEM((2, rows, units), f32),
            pltpu.VMEM((2, rows, units), f32),
            pltpu.VMEM((2, rows, units), f32),
            pltpu.VMEM((feats, units), bf16),
            pltpu.VMEM((units, feats), bf16),
            pltpu.VMEM((rows, 384), f32),
            pltpu.VMEM((tensor - 1, rows // tensor, 384), f32),
            pltpu.VMEM((rows, feats), bf16),
            pltpu.VMEM((feats, RANK), bf16),
            pltpu.VMEM((feats, RANK), bf16),
            pltpu.VMEM((units, RANK), bf16),
            pltpu.VMEM((units, RANK), bf16),
            pltpu.VMEM((units, RANK), bf16),
            dma((7,)),
            dma((2,)), dma((2,)), dma((2,)),
            dma((steps,)), dma((steps,)), dma((steps,)), dma((steps,)), dma((steps,)),
            dma((PIECES,)), dma((PIECES,)),
            dma((3,)), dma((3,)), dma((3,)), pltpu.SemaphoreType.REGULAR,
            dma((tensor - 1,)), dma((tensor - 1,)), dma((tensor - 1,)), dma((tensor - 1,)),
        ],
        compiler_params=pltpu.CompilerParams(
            collective_id=0, has_side_effects=True, vmem_limit_bytes=61 * 1024 * 1024
        ),
    )(tokens, cotangent, gate_weight, up_weight, down_weight, pt, pc, ph, pgate, pup)


def local(
    tensor,
    tokens,
    cotangent,
    gate_weight,
    up_weight,
    down_weight,
    proj_tokens,
    proj_cotangent,
    proj_hidden,
    proj_gate,
    proj_up,
    doc_ids,
    query_grads,
):
    summed = projected_rows(
        tensor, tokens, cotangent, gate_weight, up_weight, down_weight,
        proj_tokens, proj_cotangent, proj_hidden, proj_gate, proj_up,
    )
    factors = group_factors(summed, doc_ids[0])
    return jnp.dot(
        factors,
        query_grads.astype(jnp.float32).T,
        precision=lax.Precision.HIGHEST,
        preferred_element_type=jnp.float32,
    )


def solution(mesh):
    return jax.shard_map(
        functools.partial(local, mesh.shape["tensor"]),
        mesh=mesh,
        in_specs=(
            P(("parts", "dp"), "tensor"),
            P(("parts", "dp"), "tensor"),
            P("dp", "tensor"),
            P("dp", "tensor"),
            P("tensor", "dp"),
            P("tensor", None),
            P("tensor", None),
            P("tensor", None),
            P("tensor", None),
            P("tensor", None),
            P(("parts", "dp"), None),
            P("tensor", None),
        ),
        out_specs=P(("parts", "dp"), "tensor"),
        check_vma=False,
    )
```
